32 devices in a mesh: mp: 4 (over y, x), fsdp: 8 (over z, core).
Axes of the slice: x: 2, y: 2, z: 4, core: 2. Of those that a mesh axis runs over, the one named last changes fastest.
Arguments:
- weights: bfloat16 [4, 4096, 14336], P('mp', None, 'fsdp'), may hold values from -6 to 6
- acts: bfloat16 [4, 1024, 4096], P('mp', 'fsdp'), may hold values from -6 to 6
- cotangent: bfloat16 [4, 1024, 14336], P('mp', 'fsdp'), may hold values from -0.26367188 to 0.26367188
- token_ids: int32 [4, 1024], P('mp', 'fsdp'), may hold values from 0 to 31999, as said below
Outputs:
- merged: bfloat16 [4096, 14336], P('mp', 'fsdp')
The draws below stay inside these ranges and needn't reach their ends.
Inputs may be any that keep to these rules, and one draw needn't show every extreme that they name: `token_ids`: each calibration sequence of 512 tokens holds live ids of 1 to 31999 first and then padding ids 0, at most 256 of them.
All inputs are finite; a program needn't handle non-finite values.
Results may differ from the reference program's by a relative error of at most 0.001.
Values may be sent and summed in bfloat16 or wider, within the bound.
A program may use at most 192 MiB of HBM per device.

```python
import jax
import jax.numpy as jnp
from jax import lax

DW = 4096
FFW = 14336
SEQ = 512
SEQS = 2
VOCAB = 32000
TOKENS = 1024
MODELS = 4


def draw_token_ids(key, part):
    first_key, second_key = jax.random.split(jax.random.fold_in(key, 17))
    lengths = jax.random.randint(first_key, (MODELS, SEQS, 1), SEQ // 2, SEQ + 1)
    positions = jnp.arange(SEQ, dtype=jnp.int32)[None, None, :]
    values = jax.random.randint(second_key, (MODELS, SEQS, SEQ), 1, VOCAB)
    return jnp.where(positions < lengths, values, 0).reshape(MODELS, TOKENS).astype(jnp.int32)


def level_of(rng, dims, cuts, low, high):
    factor_of, own = 1.0, jax.random.fold_in(rng, 6)
    for dim, blocks in cuts:
        steps = jnp.exp(jax.random.uniform(jax.random.fold_in(own, dim), (blocks,), jnp.float32, low / len(cuts), high / len(cuts)))
        factor_of = factor_of * jnp.repeat(steps, dims[dim] // blocks).reshape([-1 if axis == dim else 1 for axis in range(len(dims))])
    return factor_of


def centred(own_key, shape, width, reach, cuts=(), kind=jnp.bfloat16):
    loudness = level_of(own_key, shape, cuts, -0.22, 0.18) if cuts else 1.0
    result = jax.random.normal(own_key, shape, jnp.float32) * width * loudness
    return jnp.minimum(jnp.maximum(result, -reach), reach).astype(kind)


def setup_inputs(seed: int = 0) -> dict:
    key_of = jax.random.split(jax.random.key(seed), 5)
    weights = centred(key_of[0], (MODELS, DW, FFW), 1.0, 6.0, ((0, 4), (2, 8)))
    acts = centred(key_of[1], (MODELS, TOKENS, DW), 1.0, 6.0, ((0, 4), (1, 8)))
    cotangent = centred(key_of[2], (MODELS, TOKENS, FFW), (1.0 / SEQ ** 0.5), 0.26367188, ((0, 4), (1, 8)))
    token_ids = draw_token_ids(jax.random.fold_in(key_of[4], 71), 0)
    return {"weights": weights, "acts": acts, "cotangent": cotangent, "token_ids": token_ids}


damping = 0.1


def reference(weights, acts, cotangent, token_ids):
    def add_model(totals, inputs):
        numerator, denominator = totals
        model_weights, model_acts, model_grads, model_ids = inputs
        live_rows = (model_ids > 0).astype(jnp.bfloat16)
        masked = model_grads * live_rows[:, None]
        fisher = jnp.zeros((DW, FFW), jnp.float32)
        for sequence in range(SEQS):
            acts_part = model_acts[sequence * SEQ:(sequence + 1) * SEQ]
            grads_part = masked[sequence * SEQ:(sequence + 1) * SEQ]
            grads = jnp.dot(acts_part.T, grads_part, preferred_element_type=jnp.float32)
            fisher = fisher + grads * grads
        importance = fisher / SEQS + damping
        return (numerator + importance * model_weights.astype(jnp.float32), denominator + importance), None

    start = (jnp.zeros((DW, FFW), jnp.float32), jnp.zeros((DW, FFW), jnp.float32))
    (numerator, denominator), _ = lax.scan(add_model, start, (weights, acts, cotangent, token_ids))
    return (numerator / denominator).astype(jnp.bfloat16)
```

```python
import functools

import jax
import jax.numpy as jnp
from jax import lax
from jax.experimental import pallas as pl
from jax.experimental.pallas import tpu as pltpu
from jax.sharding import PartitionSpec as P

SEQS = 2
EARLY = 2


damping = 0.1


def remote(src, dst, send_sem, recv_sem, device):
    return pltpu.make_async_remote_copy(
        src_ref=src,
        dst_ref=dst,
        send_sem=send_sem,
        recv_sem=recv_sem,
        device_id=device,
        device_id_type=pl.DeviceIdType.MESH,
    )


def kernel(
    nm, nf, chunk, tile,
    w_ref, a_ref, g_ref, out_ref,
    acts, grads, wbuf, turned, obuf,
    am_send, am_recv, az_send, az_recv, as_send, as_recv,
    gf_send, gf_recv, gm_send, gm_recv, gr_send, w_send, w_recv, local_sem, out_sem,
):
    me, mine = lax.axis_index("mp"), lax.axis_index("fsdp")
    tok, cols = a_ref.shape[0], w_ref.shape[1]
    rows = w_ref.shape[0] // nm
    chunks = rows // chunk
    seq = nf * tok // SEQS
    sibling = mine + 1 - 2 * (mine % 2)
    relayed = nm == 4
    across, up = me + 1 - 2 * (me % 2), me + 2 - 4 * (me // 2)

    def model(d):
        return lax.rem(me + d, nm)

    def peer(d):
        return lax.rem(mine + d, nf)

    def tokens(f):
        return pl.ds(pl.multiple_of(f * tok, tok), tok)

    def acts_part(f):
        return acts.at[:, tokens(f), :]

    def grads_part(m, f):
        return grads.at[m, tokens(f), :]

    own = [
        pltpu.make_async_copy(
            a_ref.at[:, pl.ds(pl.multiple_of(me * rows, rows), rows)],
            acts.at[me, tokens(mine), :], local_sem.at[0]),
        pltpu.make_async_copy(
            g_ref.at[:, pl.ds(pl.multiple_of(mine * cols, cols), cols)],
            grads_part(me, mine), local_sem.at[1]),
        pltpu.make_async_copy(
            w_ref.at[pl.ds(pl.multiple_of(me * rows, rows), rows), :],
            wbuf.at[me], local_sem.at[2]),
    ]
    for copy in own:
        copy.start()

    barrier = pltpu.get_barrier_semaphore()
    for d in range(1, nm):
        pl.semaphore_signal(barrier, inc=1, device_id=(model(d), mine), device_id_type=pl.DeviceIdType.MESH)
    for d in range(1, nf):
        pl.semaphore_signal(barrier, inc=1, device_id=(me, peer(d)), device_id_type=pl.DeviceIdType.MESH)
    pl.semaphore_wait(barrier, nm + nf - 2)

    sent = []

    def start(copy):
        copy.start()
        sent.append(copy)

    for d in range(1, nm):
        j = model(d)
        start(remote(
            a_ref.at[:, pl.ds(pl.multiple_of(j * rows, rows), rows)],
            acts.at[me, tokens(mine), :], am_send.at[d], am_recv.at[me], (j, mine)))
    for d in range(1, nf):
        f = peer(d)
        start(remote(
            g_ref.at[:, pl.ds(pl.multiple_of(f * cols, cols), cols)],
            grads_part(me, mine), gf_send.at[d], gf_recv.at[mine], (me, f)))

    def send_weights(k):
        for d in range(1, nm):
            j = model(d)
            start(remote(
                w_ref.at[pl.ds(pl.multiple_of(j * rows + k * chunk, chunk), chunk), :],
                wbuf.at[me, pl.ds(k * chunk, chunk), :], w_send.at[d, k], w_recv.at[me, k], (j, mine)))

    for k in range(min(EARLY, chunks)):
        send_weights(k)

    def spread(f):
        part = grads_part(me, f)
        if relayed:
            start(remote(part, part, gm_send.at[0, f], gm_recv.at[me, f], (across, mine)))
            start(remote(part, part, gm_send.at[1, f], gm_recv.at[me, f], (up, mine)))
        else:
            for d in range(1, nm):
                start(remote(part, part, gm_send.at[d, f], gm_recv.at[me, f], (model(d), mine)))

    def arrived(m, f):
        part = grads_part(m, f)
        remote(part, part, gm_send.at[0, f], gm_recv.at[m, f], (m, mine)).wait_recv()

    def relay(f):
        odd = f % 2
        source = odd * up + (1 - odd) * across
        target = odd * across + (1 - odd) * up
        arrived(source, f)
        part = grads_part(source, f)
        start(remote(part, part, gr_send.at[f], gm_recv.at[source, f], (target, mine)))

    own[1].wait()
    spread(mine)

    own[0].wait()
    for d in range(1, nm):
        m = model(d)
        part = acts.at[m, tokens(mine), :]
        remote(part, part, am_send.at[d], am_recv.at[m], (m, mine)).wait_recv()
    start(remote(acts_part(mine), acts_part(mine), as_send.at[0], as_recv.at[mine], (me, sibling)))
    for d in range(1, nf // 2):
        start(remote(acts_part(mine), acts_part(mine), az_send.at[d], az_recv.at[mine], (me, peer(2 * d))))

    order = [nf - d for d in range(1, nf)]
    previous = mine
    for d in order:
        f = peer(d)
        part = grads_part(me, f)
        remote(part, part, gf_send.at[d], gf_recv.at[f], (me, f)).wait_recv()
        spread(f)
        if relayed:
            relay(previous)
        previous = f
    if relayed:
        relay(previous)

    for k in range(min(EARLY, chunks), chunks):
        send_weights(k)

    for d in range(1, nf // 2):
        f = lax.rem(mine + nf - 2 * d, nf)
        part = acts_part(f)
        remote(part, part, az_send.at[d], az_recv.at[f], (me, f)).wait_recv()
        start(remote(part, part, as_send.at[d], as_recv.at[f], (me, sibling)))
    for d in range(nf // 2):
        f = lax.rem(sibling + 2 * d, nf)
        part = acts_part(f)
        remote(part, part, as_send.at[d], as_recv.at[f], (me, sibling)).wait_recv()

    for d in range(nf):
        f = peer(d)
        if relayed:
            odd = f % 2
            arrived(odd * across + (1 - odd) * up, f)
            arrived(nm - 1 - me, f)
        else:
            for e in range(1, nm):
                arrived(model(e), f)
    own[2].wait()

    outs = []
    for k in range(chunks):
        here = pl.ds(k * chunk, chunk)
        for m in range(nm):
            turned[m] = acts[m, :, k * chunk:(k + 1) * chunk].T
        for d in range(1, nm):
            m = model(d)
            part = wbuf.at[m, here, :]
            remote(part, part, w_send.at[d, k], w_recv.at[m, k], (m, mine)).wait_recv()
        if k >= 2:
            outs[k - 2].wait()
        slot = k % 2

        @pl.loop(0, cols // tile)
        def _(c):
            span = pl.ds(pl.multiple_of(c * tile, tile), tile)
            numerator = jnp.zeros((chunk, tile), jnp.float32)
            denominator = jnp.zeros((chunk, tile), jnp.float32)
            for m in range(nm):
                fisher = jnp.zeros((chunk, tile), jnp.float32)
                for s in range(SEQS):
                    g = jnp.dot(
                        turned[m, :, s * seq:(s + 1) * seq],
                        grads[m, s * seq:(s + 1) * seq, span],
                        preferred_element_type=jnp.float32)
                    fisher = fisher + g * g
                importance = fisher / SEQS + damping
                numerator = numerator + importance * wbuf[m, here, span].astype(jnp.float32)
                denominator = denominator + importance
            obuf[slot, :, span] = (numerator / denominator).astype(jnp.bfloat16)

        copy = pltpu.make_async_copy(obuf.at[slot], out_ref.at[here, :], out_sem.at[slot])
        copy.start()
        outs.append(copy)
    for copy in outs[-2:]:
        copy.wait()
    for copy in sent:
        copy.wait_send()


def fit(size, most, unit):
    return max(t for t in range(unit, most + 1, unit) if size % t == 0)


def per_device(nm, nf, weights, acts, cotangent, token_ids):
    live_rows = (token_ids[0] > 0).astype(jnp.bfloat16)
    masked = acts[0] * live_rows[:, None]
    _, depth, cols = weights.shape
    rows, tok = depth // nm, acts.shape[1]
    chunk, tile = fit(rows, 256, 16), fit(cols, 256, 128)
    chunks = rows // chunk
    dma = pltpu.SemaphoreType.DMA
    bf16 = jnp.bfloat16
    return pl.pallas_call(
        functools.partial(kernel, nm, nf, chunk, tile),
        out_shape=jax.ShapeDtypeStruct((rows, cols), bf16),
        in_specs=[pl.BlockSpec(memory_space=pl.ANY)] * 3,
        out_specs=pl.BlockSpec(memory_space=pl.ANY),
        scratch_shapes=[
            pltpu.VMEM((nm, nf * tok, rows), bf16),
            pltpu.VMEM((nm, nf * tok, cols), bf16),
            pltpu.VMEM((nm, rows, cols), bf16),
            pltpu.VMEM((nm, chunk, nf * tok), bf16),
            pltpu.VMEM((2, chunk, cols), bf16),
            dma((nm,)), dma((nm,)),
            dma((nf,)), dma((nf,)), dma((nf,)), dma((nf,)),
            dma((nf,)), dma((nf,)),
            dma((nm, nf)), dma((nm, nf)), dma((nf,)),
            dma((nm, chunks)), dma((nm, chunks)),
            dma((3,)), dma((2,)),
        ],
        compiler_params=pltpu.CompilerParams(
            collective_id=0, has_side_effects=True, vmem_limit_bytes=58 * 1024 * 1024
        ),
        cost_estimate=pl.CostEstimate(
            flops=2 * nm * nf * tok * rows * cols,
            bytes_accessed=2 * (depth * cols + tok * depth + nf * tok * cols + rows * cols),
            transcendentals=0),
    )(weights[0], masked, cotangent[0])


def solution(mesh):
    return jax.shard_map(
        functools.partial(per_device, mesh.shape["mp"], mesh.shape["fsdp"]),
        mesh=mesh,
        in_specs=(
            P("mp", None, "fsdp"),
            P("mp", "fsdp", None),
            P("mp", "fsdp", None),
            P("mp", "fsdp"),
        ),
        out_specs=P("mp", "fsdp"),
        check_vma=False,
    )
```
